512 devices in a mesh: rep: 32 (over z, y_hi), fsdp: 16 (over x, y_lo, core).
Axes of the slice: x: 4, y: 4 (y_hi: 2, y_lo: 2; y = y_hi * 2 + y_lo), z: 16, core: 2. Of those that a mesh axis runs over, the one named last changes fastest.
Arguments:
- tokens: bfloat16 [114688, 8192], P(('rep', 'fsdp')), may hold values from -24 to 24
- cotangent: bfloat16 [114688, 256], P(('rep', 'fsdp')), may hold values from -6 to 6
- weight: float32 [32, 8192, 256], P('rep', 'fsdp'), may hold values from -6 to 6
- gain: float32 [32, 8192], P('rep', 'fsdp'), may hold values from 0.5 to 1.5
- step: int32 [], replicated, may hold values from 0 to 999
Outputs:
- keys_values: bfloat16 [114688, 256], P(('rep', 'fsdp'))
- new_weight: float32 [32, 8192, 256], P('rep', 'fsdp')
- new_gain: float32 [32, 8192], P('rep', 'fsdp')
The draws below stay inside these ranges and needn't reach their ends.
All inputs are finite; a program needn't handle non-finite values.
Results may differ from the reference program's by a relative error of at most 0.0065.
Values may be sent and summed in bfloat16 or wider, within the bound.
A program may use at most 64 MiB of HBM per device.

```python
import jax
import jax.numpy as jnp
from jax import lax

D = 8192
HEAD = 128
TOK_DEV = 224
KV = 256
TOKENS = 114688
N_REP = 32
N_FSDP = 16


def spiked(result, own_key, source, target, blocks, factor):
    owner, partner = [(jnp.arange(result.shape[position]) // (result.shape[position] // blocks)).reshape([-1 if axis == position else 1 for axis in range(result.ndim)]) for position in (source, target)]
    chosen = jax.random.permutation(own_key, blocks)[partner]
    strong = (owner == chosen) | (owner == (partner + blocks // 2) % blocks)
    return jnp.where(strong, factor * result, result)


def level_of(stream_key, extent, split, smallest, high):
    loudness = 1.0
    for axis_at, shards_of in split:
        steps = jax.random.uniform(jax.random.fold_in(jax.random.fold_in(stream_key, 6), axis_at), (shards_of,), jnp.float32, smallest / len(split), high / len(split))
        loudness = loudness * jnp.repeat(jnp.exp(steps), extent[axis_at] // shards_of).reshape((-1,) + (1,) * (len(extent) - 1 - axis_at))
    return loudness


def scatter_about(key, dims, scale, limit, split=(), held_as=jnp.bfloat16):
    result = scale * jax.random.normal(key, dims, jnp.float32)
    if split:
        result = result * level_of(key, dims, split, -0.22, 0.18)
    return jnp.clip(result, -limit, limit).astype(held_as)


def bell_draw_with(stream_key, shape, spread, limit, split, heavy, kind=jnp.bfloat16):
    drawn = spread * jax.random.normal(stream_key, shape, jnp.float32)
    if split:
        drawn = drawn * level_of(stream_key, shape, split, -0.22, 0.18)
    return jnp.clip(spiked(drawn, jax.random.fold_in(stream_key, 3), *heavy), -limit, limit).astype(kind)


def setup_inputs(seed: int = 0) -> dict:
    keys = jax.random.split(jax.random.key(seed), 6)
    tokens = bell_draw_with(keys[0], (TOKENS, D), 1.0, 24.0, ((0, 512),), (0, 1, 512, 6.0))
    cotangent = scatter_about(keys[1], (TOKENS, KV), 1.0, 6.0, ((0, 512),))
    weight = scatter_about(keys[2], (N_REP, D, KV), 1.0, 6.0, ((0, 32), (1, 16)), jnp.float32)
    gain = jnp.clip(1.0 + 0.1 * jax.random.normal(keys[3], (N_REP, D), jnp.float32), 0.5, 1.5)
    step = jax.random.randint(keys[4], (), 0, 1000).astype(jnp.int32)
    return {"tokens": tokens, "cotangent": cotangent, "weight": weight, "gain": gain, "step": step}


learn_rate = 0.25
gain_rate = 0.01

def reference(tokens, cotangent, weight, gain, step):
    scale = D ** (-0.5)
    levels = N_REP.bit_length() - 1
    rows = TOK_DEV * N_FSDP
    token_sets = tokens.reshape(N_REP, rows, D)
    cot_sets = cotangent.reshape(N_REP, rows, 2 * HEAD)

    def one_replica(items):
        inputs, grads_out, master, gains = items
        w_half = master.astype(jnp.bfloat16)
        gain_gradient_half = lax.optimization_barrier(gains.astype(jnp.bfloat16)).astype(jnp.float32)
        value_rows = inputs.astype(jnp.float32)
        normalized_input = value_rows * lax.rsqrt(lax.optimization_barrier(jnp.mean(value_rows * value_rows, -1, keepdims=True)) + 1e-05)
        hidden_state = (normalized_input * gain_gradient_half).astype(jnp.bfloat16)
        outputs = (jnp.dot(hidden_state, w_half, preferred_element_type=jnp.float32) * scale).astype(jnp.bfloat16)
        hidden_gradient = jnp.dot(grads_out, w_half.T, preferred_element_type=jnp.float32) * scale
        gain_gradient = lax.optimization_barrier(jnp.sum(hidden_gradient * normalized_input, 0))
        blocks_h = hidden_state.reshape(N_FSDP, TOK_DEV, D).astype(jnp.float32)
        blocks_c = grads_out.reshape(N_FSDP, TOK_DEV, 2 * HEAD).astype(jnp.float32)
        partial_sums = jnp.einsum('btd,btk->bdk', blocks_h, blocks_c) * scale
        partial_sums = lax.optimization_barrier(partial_sums.astype(jnp.bfloat16)).astype(jnp.float32)
        grad_weight = lax.optimization_barrier(jnp.sum(partial_sums, 0))
        return (outputs, master - learn_rate * grad_weight, gains - gain_rate * gain_gradient)
    outputs, upd_weight, upd_gain = lax.map(one_replica, (token_sets, cot_sets, weight, gain))
    distance = jnp.left_shift(jnp.int32(1), (step % levels).astype(jnp.int32))
    source = (jnp.arange(N_REP, dtype=jnp.int32) - distance) % N_REP
    new_weight = 0.5 * (upd_weight + upd_weight[source])
    new_gain = 0.5 * (upd_gain + upd_gain[source])
    return (outputs.reshape(N_REP * rows, 2 * HEAD), new_weight, new_gain)
```

```python
import jax
import jax.numpy as jnp
from jax import lax
from jax.sharding import PartitionSpec as P

learn_rate = 0.25
gain_rate = 0.01


def from_behind(block, axis, distance):
    devices = range(lax.axis_size(axis))
    route = [((i - distance) % len(devices), i) for i in devices]
    return lax.ppermute(block, axis, route)


def late_mover(bit):
    return lambda block: from_behind(block, "rep", 1 << bit)


def body(tokens, cotangent, weight, gain, step):
    width = tokens.shape[1]
    scale = width ** (-0.5)
    levels = lax.axis_size("rep").bit_length() - 1
    master, gains = weight[0], gain[0]
    rows, columns = master.shape
    which = step % levels

    w_half = master.astype(jnp.bfloat16).astype(jnp.float32)
    g_half = gains.astype(jnp.bfloat16).astype(jnp.float32)
    whole_w = lax.all_gather(
        (w_half * g_half[:, None]).astype(jnp.bfloat16), "fsdp", axis=0, tiled=True
    )
    values = tokens.astype(jnp.float32)
    inverse = lax.rsqrt(jnp.mean(values * values, -1, keepdims=True) + 1e-05) * scale
    scaled = (cotangent.astype(jnp.float32) * inverse).astype(jnp.bfloat16)
    part = lax.dot_general(
        tokens, scaled, (((0,), (0,)), ((), ())), preferred_element_type=jnp.float32
    ).astype(jnp.bfloat16)
    product = lax.psum_scatter(part, "fsdp", scatter_dimension=0, tiled=True).astype(jnp.float32)
    keys_values = (
        jnp.dot(tokens, whole_w, preferred_element_type=jnp.float32) * inverse
    ).astype(jnp.bfloat16)
    upd_weight = master - learn_rate * (g_half[:, None] * product)
    upd_gain = gains - gain_rate * jnp.sum(w_half * product, 1)
    gain_rows = rows // columns
    payload = jnp.concatenate(
        [upd_weight, upd_gain.reshape(gain_rows, columns), jnp.zeros((16 - gain_rows, columns))], 0
    ).astype(jnp.bfloat16)
    other = lax.switch(which, [late_mover(bit) for bit in range(levels)], payload)
    other = other.astype(jnp.float32)
    new_weight = 0.5 * (upd_weight + other[:rows])
    new_gain = 0.5 * (upd_gain + other[rows : rows + gain_rows].reshape(rows))
    return (keys_values, new_weight[None], new_gain[None])


def solution(mesh):
    return jax.shard_map(
        body,
        mesh=mesh,
        in_specs=(
            P(("rep", "fsdp"), None),
            P(("rep", "fsdp"), None),
            P("rep", "fsdp", None),
            P("rep", "fsdp"),
            P(),
        ),
        out_specs=(P(("rep", "fsdp"), None), P("rep", "fsdp", None), P("rep", "fsdp")),
        check_vma=False,
    )
```

```python
import functools

import jax
import jax.numpy as jnp
from jax import lax
from jax.experimental import pallas as pl
from jax.experimental.pallas import tpu as pltpu
from jax.sharding import PartitionSpec as P

learn_rate = 0.25
gain_rate = 0.01
MESH = pl.DeviceIdType.MESH
F32, BF16 = jnp.float32, jnp.bfloat16
N_SUB = 2
MESSAGES = 96


def kernel(
    distance, n_rep, tokens, cotangent, weight, gain, kv_out, weight_out, gain_out,
    tok, tok_rest, cot, master, gains, gain_cols, scaled, inverse, part_a, part_b, whole_w,
    from_a1, from_a2, from_a3, from_b1, from_b2, from_b3, payload, other, upd, upd_gain,
    total, from_sibling, local_sem, send_sem, recv_sem,
):
    rep, fsdp = lax.axis_index("rep"), lax.axis_index("fsdp")
    n_fsdp = lax.axis_size("fsdp")
    x, y, core = fsdp // 4, (fsdp // 2) % 2, fsdp % 2
    mate = 1 - y
    sibling = (rep, fsdp + 1 - 2 * core)
    across = (rep, fsdp + 2 - 4 * y)
    right = (rep, (fsdp + 4) % n_fsdp)
    left = (rep, (fsdp + n_fsdp - 4) % n_fsdp)
    ahead = ((rep + distance) % n_rep, fsdp)
    behind = ((rep + n_rep - distance) % n_rep, fsdp)
    at = [(x + j) % 4 for j in range(4)]
    rows_y = (y, mate)
    n_tok = cotangent.shape[0]
    width = tokens.shape[1]
    shard, kv = master.shape
    sub = shard // N_SUB
    half = sub // 2
    scale = width**-0.5

    barrier = pltpu.get_barrier_semaphore()
    for partner in (sibling, across, right, left, ahead, behind):
        pl.semaphore_signal(barrier, inc=1, device_id=partner, device_id_type=MESH)

    def load(source, target, index):
        copy = pltpu.make_async_copy(source, target, local_sem.at[index])
        copy.start()
        return copy

    load_w = load(weight.at[0], master, 0)
    load_g = load(gain, gains, 1)
    load_c = load(cotangent, cot, 2)
    load_t = []
    for block in range(8):
        for mine in (True, False):
            column = 1024 * block + 512 * (core if mine else 1 - core)
            source = tokens.at[:, pl.ds(pl.multiple_of(column, 512), 512)]
            target = tok.at[block // 2, block % 2, pl.ds(0, n_tok)] if mine else tok_rest.at[block]
            load_t.append((load(source, target, 3 + len(load_t)), target))

    names = {}
    sent = []

    def message(name, source, target, device):
        index = names.setdefault(name, len(names))
        assert index < MESSAGES
        return pltpu.make_async_remote_copy(
            src_ref=source, dst_ref=target, send_sem=send_sem.at[index],
            recv_sem=recv_sem.at[index], device_id=device, device_id_type=MESH,
        )

    def send(name, source, target, device):
        copy = message(name, source, target, device)
        copy.start()
        sent.append(copy)

    def receive(name, target, device):
        message(name, target, target, device).wait_recv()

    load_w.wait()
    load_g.wait()
    gb_row = gains[...].astype(BF16).astype(F32)
    for k in range(shard // 128):
        block = slice(128 * k, 128 * k + 128)
        column = jnp.broadcast_to(gb_row[:, block], (128, 128)).T
        gain_cols[block] = column
        wb = master[block].astype(BF16).astype(F32)
        whole_w[x, y, k // 2, k % 2] = (wb * jnp.concatenate([column, column], 1)).astype(BF16)

    pl.semaphore_wait(barrier, 6)

    for name, device in (("g1y", across), ("g1r", right), ("g1l", left)):
        send(name, whole_w.at[x, y], whole_w.at[x, y], device)
    order = [(j, q) for j in (2, 1, 3, 0) for q in (1, 0)]
    theirs = pl.ds(n_tok, n_tok)
    for s in range(N_SUB):
        for j, q in order:
            column = 512 * (4 * at[j] + 2 * rows_y[q] + 1 - core) + sub * s
            send(
                f"t{s}{j}{q}", tokens.at[:, pl.ds(pl.multiple_of(column, sub), sub)],
                tok.at[at[j], rows_y[q], theirs, pl.ds(sub * s, sub)], sibling,
            )

    squares = jnp.zeros((n_tok, 128), F32)
    for copy, target in load_t:
        copy.wait()
        for k in range(4):
            value = target[:, 128 * k : 128 * k + 128].astype(F32)
            squares = squares + value * value
    inverse_now = lax.rsqrt(jnp.sum(squares, 1, keepdims=True) * (1.0 / width) + 1e-05) * scale
    inverse[...] = jnp.broadcast_to(inverse_now, (n_tok, 128))
    load_c.wait()
    scaled[0:n_tok] = (cot[...].astype(F32) * inverse_now).astype(BF16)
    send("cot", scaled.at[pl.ds(0, n_tok)], scaled.at[theirs], sibling)
    receive("cot", scaled.at[theirs], sibling)

    for s in range(N_SUB):
        columns = pl.ds(sub * s, sub)
        for j, q in order:
            target = tok.at[at[j], rows_y[q], theirs, columns]
            receive(f"t{s}{j}{q}", target, sibling)
            product = lax.dot_general(
                tok[at[j], rows_y[q], :, columns], scaled[...], (((0,), (0,)), ((), ())),
                preferred_element_type=F32,
            ).astype(BF16)
            part_a[at[j], s, rows_y[q]] = product[:half].reshape(2, half // 2, kv)
            part_b[at[j], s, rows_y[q]] = product[half:].reshape(2, half // 2, kv)
            if q == 1:
                send(f"b1{s}{j}", part_b.at[at[j], s, mate], from_b1.at[s, j], across)
            elif j == 2:
                send(f"a1r{s}", part_a.at[at[2], s, :, 0], from_a1.at[s, 0], right)
                send(f"a1l{s}", part_a.at[at[2], s, :, 1], from_a1.at[s, 1], left)

    def add(target, *sources):
        value = target[...].astype(F32)
        for source in sources:
            value = value + source[...].astype(F32)
        target[...] = value.astype(BF16)

    def step_a2(s):
        receive(f"a1r{s}", from_a1.at[s, 0], left)
        add(part_a.at[at[1], s, :, 0], from_a1.at[s, 0])
        send(f"a2r{s}", part_a.at[at[1], s], from_a2.at[s, 0], right)
        receive(f"a1l{s}", from_a1.at[s, 1], right)
        add(part_a.at[at[3], s, :, 1], from_a1.at[s, 1])
        send(f"a2l{s}", part_a.at[at[3], s], from_a2.at[s, 1], left)

    def step_b2(s):
        receive(f"b1{s}2", from_b1.at[s, 2], across)
        add(part_b.at[at[2], s, y], from_b1.at[s, 2])
        send(f"b2r{s}", part_b.at[at[2], s, y, 0], from_b2.at[s, 0], right)
        send(f"b2l{s}", part_b.at[at[2], s, y, 1], from_b2.at[s, 1], left)

    def step_b3(s):
        receive(f"b1{s}1", from_b1.at[s, 1], across)
        receive(f"b2r{s}", from_b2.at[s, 0], left)
        add(part_b.at[at[1], s, y, 0], from_b1.at[s, 1, 0], from_b2.at[s, 0])
        add(part_b.at[at[1], s, y, 1], from_b1.at[s, 1, 1])
        send(f"b3r{s}", part_b.at[at[1], s, y], from_b3.at[s, 0], right)
        receive(f"b1{s}3", from_b1.at[s, 3], across)
        receive(f"b2l{s}", from_b2.at[s, 1], right)
        add(part_b.at[at[3], s, y, 0], from_b1.at[s, 3, 0])
        add(part_b.at[at[3], s, y, 1], from_b1.at[s, 3, 1], from_b2.at[s, 1])
        send(f"b3l{s}", part_b.at[at[3], s, y], from_b3.at[s, 1], left)

    def step_a3(s):
        receive(f"a2r{s}", from_a2.at[s, 0], left)
        receive(f"a2l{s}", from_a2.at[s, 1], right)
        add(part_a.at[at[0], s, mate], from_a2.at[s, 0, mate], from_a2.at[s, 1, mate])
        send(f"a3{s}", part_a.at[at[0], s, mate], from_a3.at[s], across)

    def update(s, which, sources):
        product = sources[0][...].astype(F32)
        for source in sources[1:]:
            product = product + source[...].astype(F32)
        product = product.reshape(half, kv)
        start = sub * s + half * which
        rows = slice(start, start + half)
        own = master[rows]
        column = gain_cols[rows]
        new = own - learn_rate * (product * jnp.concatenate([column, column], 1))
        upd[rows] = new
        payload[s, which, 0:half] = new.astype(BF16)
        share = own.astype(BF16).astype(F32) * product
        gain_gradient = jnp.sum((share[:, :128] + share[:, 128:]).T, 0, keepdims=True)
        new_gain = gains[:, rows] - gain_rate * gain_gradient
        upd_gain[:, rows] = new_gain
        payload[s, which, half : half + 16] = jnp.broadcast_to(
            jnp.concatenate([new_gain, new_gain], 1), (16, kv)
        ).astype(BF16)
        send(f"p{s}{which}", payload.at[s, which], other.at[s, which], ahead)

    def step_b4(s):
        receive(f"b1{s}0", from_b1.at[s, 0], across)
        receive(f"b3r{s}", from_b3.at[s, 0], left)
        receive(f"b3l{s}", from_b3.at[s, 1], right)
        update(s, 1, [part_b.at[at[0], s, y], from_b1.at[s, 0], from_b3.at[s, 0], from_b3.at[s, 1]])

    def step_a4(s):
        receive(f"a3{s}", from_a3.at[s], across)
        update(
            s, 0,
            [part_a.at[at[0], s, y], from_a2.at[s, 0, y], from_a2.at[s, 1, y], from_a3.at[s]],
        )

    def average(s, which):
        receive(f"p{s}{which}", other.at[s, which], behind)
        start = sub * s + half * which
        rows = slice(start, start + half)
        weight_out[0, rows] = 0.5 * (upd[rows] + other[s, which, 0:half].astype(F32))
        theirs_now = other[s, which, half : half + 16].astype(F32)[0:1, :half]
        gain_out[:, rows] = 0.5 * (upd_gain[:, rows] + theirs_now)

    def forward(j, q, first=False):
        value = jnp.dot(
            tok[at[j], rows_y[q]], whole_w[at[j], rows_y[q]].reshape(shard, kv),
            preferred_element_type=F32,
        )
        total[...] = value if first else total[...] + value

    def gather_2():
        receive("g1y", whole_w.at[x, mate], across)
        send("g2pr", whole_w.at[x, mate, 0], whole_w.at[x, mate, 0], right)
        send("g2pl", whole_w.at[x, mate, 0], whole_w.at[x, mate, 0], left)
        receive("g1r", whole_w.at[at[3], y], left)
        send("g2r", whole_w.at[at[3], y, :, 0], whole_w.at[at[3], y, :, 0], right)
        send("g2yl", whole_w.at[at[3], y, 1], whole_w.at[at[3], y, 1], across)
        receive("g1l", whole_w.at[at[1], y], right)
        send("g2l", whole_w.at[at[1], y, :, 1], whole_w.at[at[1], y, :, 1], left)
        send("g2yr", whole_w.at[at[1], y, 1], whole_w.at[at[1], y, 1], across)

    def gather_3():
        receive("g2r", whole_w.at[at[2], y, :, 0], left)
        receive("g2l", whole_w.at[at[2], y, :, 1], right)
        send("g3y", whole_w.at[at[2], y, 1], whole_w.at[at[2], y, 1], across)
        receive("g2pr", whole_w.at[at[3], mate, 0], left)
        send("g3r", whole_w.at[at[3], mate, 0, 0], whole_w.at[at[3], mate, 0, 0], right)
        receive("g2pl", whole_w.at[at[1], mate, 0], right)
        send("g3l", whole_w.at[at[1], mate, 0, 1], whole_w.at[at[1], mate, 0, 1], left)

    step_a2(0)
    step_b2(0)
    step_a2(1)
    step_b3(0)
    step_b2(1)
    step_a3(0)
    step_b4(0)
    step_b3(1)
    step_a3(1)
    gather_2()
    forward(0, 0, True)
    step_a4(0)
    step_b4(1)
    step_a4(1)
    forward(0, 1)
    forward(1, 0)
    gather_3()
    forward(3, 0)
    forward(2, 0)
    receive("g2yl", whole_w.at[at[3], mate, 1], across)
    forward(3, 1)
    receive("g2yr", whole_w.at[at[1], mate, 1], across)
    forward(1, 1)
    receive("g3r", whole_w.at[at[2], mate, 0, 0], left)
    receive("g3l", whole_w.at[at[2], mate, 0, 1], right)
    receive("g3y", whole_w.at[at[2], mate, 1], across)
    forward(2, 1)
    send("out", total.at[theirs], from_sibling, sibling)
    average(0, 1)
    average(0, 0)
    average(1, 1)
    average(1, 0)
    receive("out", from_sibling, sibling)
    factor = inverse[...]
    kv_out[...] = (
        (total[0:n_tok] + from_sibling[...]) * jnp.concatenate([factor, factor], 1)
    ).astype(BF16)
    for copy in sent:
        copy.wait_send()


def step_at(distance, collective, n_rep, tokens, cotangent, weight, gain):
    n_tok, width = tokens.shape
    _, shard, kv = weight.shape
    quarter = shard // N_SUB // 4
    half = 2 * quarter
    any_space = pl.BlockSpec(memory_space=pl.ANY)
    vmem = pl.BlockSpec(memory_space=pltpu.VMEM)
    return pl.pallas_call(
        functools.partial(kernel, distance, n_rep),
        out_shape=(
            jax.ShapeDtypeStruct((n_tok, kv), BF16),
            jax.ShapeDtypeStruct(weight.shape, F32),
            jax.ShapeDtypeStruct(gain.shape, F32),
        ),
        in_specs=[any_space] * 4,
        out_specs=(vmem, vmem, vmem),
        scratch_shapes=[
            pltpu.VMEM((4, 2, 2 * n_tok, shard), BF16),
            pltpu.VMEM((8, n_tok, shard), BF16),
            pltpu.VMEM((n_tok, kv), BF16),
            pltpu.VMEM((shard, kv), F32),
            pltpu.VMEM((1, shard), F32),
            pltpu.VMEM((shard, 128), F32),
            pltpu.VMEM((2 * n_tok, kv), BF16),
            pltpu.VMEM((n_tok, 128), F32),
            pltpu.VMEM((4, N_SUB, 2, 2, quarter, kv), BF16),
            pltpu.VMEM((4, N_SUB, 2, 2, quarter, kv), BF16),
            pltpu.VMEM((4, 2, 2, 2, shard // 4, kv), BF16),
            pltpu.VMEM((N_SUB, 2, 2, quarter, kv), BF16),
            pltpu.VMEM((N_SUB, 2, 2, 2, quarter, kv), BF16),
            pltpu.VMEM((N_SUB, 2, quarter, kv), BF16),
            pltpu.VMEM((N_SUB, 4, 2, quarter, kv), BF16),
            pltpu.VMEM((N_SUB, 2, quarter, kv), BF16),
            pltpu.VMEM((N_SUB, 2, 2, quarter, kv), BF16),
            pltpu.VMEM((N_SUB, 2, half + 16, kv), BF16),
            pltpu.VMEM((N_SUB, 2, half + 16, kv), BF16),
            pltpu.VMEM((shard, kv), F32),
            pltpu.VMEM((1, shard), F32),
            pltpu.VMEM((2 * n_tok, kv), F32),
            pltpu.VMEM((n_tok, kv), F32),
            pltpu.SemaphoreType.DMA((19,)),
            pltpu.SemaphoreType.DMA((MESSAGES,)),
            pltpu.SemaphoreType.DMA((MESSAGES,)),
        ],
        compiler_params=pltpu.CompilerParams(
            collective_id=collective, has_side_effects=True, vmem_limit_bytes=48 * 2**20
        ),
        name=f"step_{distance}",
    )(tokens, cotangent, weight, gain)


def body(tokens, cotangent, weight, gain, step):
    n_rep = lax.axis_size("rep")
    levels = n_rep.bit_length() - 1
    branches = [functools.partial(step_at, 1 << bit, bit, n_rep) for bit in range(levels)]
    return lax.switch(step % levels, branches, tokens, cotangent, weight, gain)


def solution(mesh):
    return jax.shard_map(
        body,
        mesh=mesh,
        in_specs=(
            P(("rep", "fsdp"), None),
            P(("rep", "fsdp"), None),
            P("rep", "fsdp", None),
            P("rep", "fsdp"),
            P(),
        ),
        out_specs=(P(("rep", "fsdp"), None), P("rep", "fsdp", None), P("rep", "fsdp")),
        check_vma=False,
    )
```

```python
import functools

import jax
import jax.numpy as jnp
from jax import lax
from jax.experimental import pallas as pl
from jax.experimental.pallas import tpu as pltpu
from jax.sharding import PartitionSpec as P

learn_rate = 0.25
gain_rate = 0.01
MESH = pl.DeviceIdType.MESH
F32, BF16 = jnp.float32, jnp.bfloat16
MESSAGES = 128
NEAR_STEPS = (
    "g1ya", "g1xb", "t_0_first", "t_0_rest", "norm", "scaled", "t_1", "p_0_first", "p_0_rest", "p_1", "a2_0",
    "b2_0", "a2_1", "b3_0", "b2_1", "a3_0", "b4_0", "b3_1", "a3_1", "g1xa", "g1yb", "g2b", "g2y", "g2p",
    "a4_0", "b4_1", "a4_1", "gain", "g2a", "g3y", "g3x", "f00", "f10", "f30", "f01", "f20", "f31", "f11",
    "f21", "out", "av_01", "av_00", "av_11", "av_10", "average_gain", "finish",
)
FAR_STEPS = (
    "g1xb", "t_0_first", "norm", "scaled", "g1ya", "t_0_rest", "p_0_first", "t_1", "p_0_rest", "p_1", "b2_0",
    "a2_0", "p_3", "b3_0", "a2_1", "b2_1", "a3_0", "p_2", "a2_3", "b4_0", "g1xa", "a4_0", "a3_1", "f00",
    "b3_1", "b2_2", "b2_3", "a2_2", "a4_1", "a3_3", "b3_2", "b4_1", "a3_2", "a4_3", "f30", "b3_3", "g2b",
    "g2y", "f10", "g1yb", "g2p", "a4_2", "b4_2", "b4_3", "g3y", "g2a", "gain", "f31", "f11", "g3x", "f20",
    "av_11", "f21", "av_20", "av_30", "av_21", "av_10", "f01", "out", "av_01", "av_31", "av_00",
    "average_gain", "finish",
)
NEXT = (2, (80, 80, 48, 48), (352, 160), NEAR_STEPS)
NEAR = (2, (80, 64, 48, 64), (288, 224), NEAR_STEPS)
FAR = (4, (48, 32, 16, 32), (288, 224), FAR_STEPS)


def kernel(
    distance, n_rep, plan, tokens, cotangent, weight, gain, kv_out, weight_out, gain_out,
    tok, tok_rest, cot, master, gains, gain_cols, scaled, inverse, part_a, part_b, whole_w,
    from_a1, from_a2, from_a3, from_b1, from_b2, from_b3, payload, other, share, upd, upd_gain, new_weight, new_kv,
    gain_sent, gain_other, total, from_sibling, meeting, local_sem, send_sem, recv_sem,
):
    n_sub, split, (wa_rows, wb_rows), schedule = plan
    rep, fsdp = lax.axis_index("rep"), lax.axis_index("fsdp")
    n_fsdp = lax.axis_size("fsdp")
    x, y, core = fsdp // 4, (fsdp // 2) % 2, fsdp % 2
    mate = 1 - y
    sibling = (rep, fsdp + 1 - 2 * core)
    across = (rep, fsdp + 2 - 4 * y)
    right = (rep, (fsdp + 4) % n_fsdp)
    left = (rep, (fsdp + n_fsdp - 4) % n_fsdp)
    ahead = ((rep + distance) % n_rep, fsdp)
    behind = ((rep + n_rep - distance) % n_rep, fsdp)
    at = [(x + j) % 4 for j in range(4)]
    rows_y = (y, mate)
    n_tok = cotangent.shape[0]
    width = tokens.shape[1]
    shard, kv = master.shape
    sub = shard // n_sub
    token_part = max(sub, shard // 2)
    a_rows, b_rows = split[0] + split[1], split[2] + split[3]
    a_ways = (pl.ds(0, split[0]), pl.ds(split[0], split[1]))
    b_ways = (pl.ds(0, split[2]), pl.ds(split[2], split[3]))
    wa, wb = pl.ds(0, wa_rows), pl.ds(wa_rows, wb_rows)
    wa_ways = (pl.ds(0, wa_rows // 2), pl.ds(wa_rows // 2, wa_rows // 2))
    wb_ways = (pl.ds(wa_rows, wb_rows // 2), pl.ds(wa_rows + wb_rows // 2, wb_rows // 2))
    scale = width**-0.5
    theirs = pl.ds(n_tok, n_tok)

    barrier = pltpu.get_barrier_semaphore()
    first, second = fsdp - core, fsdp - core + 1

    def greet(device):
        pl.semaphore_signal(barrier, inc=1, device_id=device, device_id_type=MESH)

    @pl.when(core == 1)
    def _():
        greet((rep, first))

    for f in ((first + 2 - 4 * y), (first + 4) % n_fsdp, (first + n_fsdp - 4) % n_fsdp):
        greet((rep, f))
    greet((ahead[0], second))
    greet((behind[0], second))

    def tell(semaphore):
        pl.semaphore_signal(semaphore, inc=1, device_id=sibling, device_id_type=MESH)

    def meet_group():
        @pl.when(core == 0)
        def _():
            pl.semaphore_wait(barrier, 7)
            tell(meeting.at[0])

        @pl.when(core == 1)
        def _():
            pl.semaphore_wait(meeting.at[0], 1)

    def meet_far():
        @pl.when(core == 1)
        def _():
            pl.semaphore_wait(barrier, 4)
            tell(meeting.at[1])

        @pl.when(core == 0)
        def _():
            pl.semaphore_wait(meeting.at[1], 1)

    def load(source, target, index):
        copy = pltpu.make_async_copy(source, target, local_sem.at[index])
        copy.start()
        return copy

    load_w = load(weight.at[0], master, 0)
    load_g = load(gain, gains, 1)
    load_c = load(cotangent, cot, 2)
    load_t = []
    for block in range(8):
        for mine in (True, False):
            column = 1024 * block + 512 * (core if mine else 1 - core)
            source = tokens.at[:, pl.ds(pl.multiple_of(column, 512), 512)]
            target = tok.at[block // 2, block % 2, pl.ds(0, n_tok)] if mine else tok_rest.at[block]
            load_t.append((load(source, target, 3 + len(load_t)), target))

    names = {}
    sent = {}
    done = set()

    def message(name, source, target, device):
        index = names.setdefault(name, len(names))
        assert index < MESSAGES
        return pltpu.make_async_remote_copy(
            src_ref=source, dst_ref=target, send_sem=send_sem.at[index],
            recv_sem=recv_sem.at[index], device_id=device, device_id_type=MESH,
        )

    def send(name, source, target, device):
        sent[name] = message(name, source, target, device)
        sent[name].start()

    def receive(name, target, device):
        if name not in done:
            done.add(name)
            message(name, target, target, device).wait_recv()

    load_w.wait()
    load_g.wait()
    gb_row = gains[...].astype(BF16).astype(F32)
    for k in range(shard // 128):
        block = slice(128 * k, 128 * k + 128)
        gain_cols[block] = jnp.broadcast_to(gb_row[:, block], (128, 128)).T
        wb_block = master[block].astype(BF16).astype(F32)
        column = gain_cols[block]
        whole_w[x, y, block] = (wb_block * jnp.concatenate([column, column], 1)).astype(BF16)

    meet_group()

    def move(name, ref, device):
        send(name, ref, ref, device)

    def gather_1y(part, rows):
        move("g1y" + part, whole_w.at[x, y, rows], across)

    def gather_1x(part, rows):
        move("g1r" + part, whole_w.at[x, y, rows], right)
        move("g1l" + part, whole_w.at[x, y, rows], left)

    def send_tokens(s, chips):
        for j, q in [(j, q) for j in chips for q in (1, 0)]:
            column = 512 * (4 * at[j] + 2 * rows_y[q] + 1 - core) + token_part * s
            send(
                f"t{s}{j}{q}", tokens.at[:, pl.ds(pl.multiple_of(column, token_part), token_part)],
                tok.at[at[j], rows_y[q], theirs, pl.ds(token_part * s, token_part)], sibling,
            )

    def norm():
        squares = jnp.zeros((n_tok, 128), F32)
        for copy, target in load_t:
            copy.wait()
            for k in range(4):
                value = target[:, 128 * k : 128 * k + 128].astype(F32)
                squares = squares + value * value
        mean = jnp.sum(squares, 1, keepdims=True) * (1.0 / width)
        inverse[...] = jnp.broadcast_to(lax.rsqrt(mean + 1e-05) * scale, (n_tok, 128))

    def scale_cotangent():
        load_c.wait()
        factor = inverse[...]
        scaled[0:n_tok] = (cot[...].astype(F32) * jnp.concatenate([factor, factor], 1)).astype(BF16)
        send("cot", scaled.at[pl.ds(0, n_tok)], scaled.at[theirs], sibling)

    def product(s, chips):
        columns = pl.ds(sub * s, sub)
        receive("cot", scaled.at[theirs], sibling)
        for j in chips:
            for q in (1, 0):
                h = sub * s // token_part
                half = pl.ds(token_part * h, token_part)
                receive(f"t{h}{j}{q}", tok.at[at[j], rows_y[q], theirs, half], sibling)
        for j in chips:
            for q in (1, 0):
                value = lax.dot_general(
                    tok[at[j], rows_y[q], :, columns], scaled[...], (((0,), (0,)), ((), ())),
                    preferred_element_type=F32,
                ).astype(BF16)
                part_a[at[j], s, rows_y[q]] = value[:a_rows]
                part_b[at[j], s, rows_y[q]] = value[a_rows:]
        for j in chips:
            send(f"b1{s}{j}", part_b.at[at[j], s, mate], from_b1.at[s, j], across)
            if j == 2:
                send(f"a1r{s}", part_a.at[at[2], s, :, a_ways[0]], from_a1.at[s, :, a_ways[0]], right)
                send(f"a1l{s}", part_a.at[at[2], s, :, a_ways[1]], from_a1.at[s, :, a_ways[1]], left)

    def add(target, *sources):
        value = target[...].astype(F32)
        for source in sources:
            value = value + source[...].astype(F32)
        target[...] = value.astype(BF16)

    def a2(s):
        go, back = a_ways
        receive(f"a1r{s}", from_a1.at[s, :, go], left)
        add(part_a.at[at[1], s, :, go], from_a1.at[s, :, go])
        send(f"a2r{s}", part_a.at[at[1], s], from_a2.at[s, 0], right)
        receive(f"a1l{s}", from_a1.at[s, :, back], right)
        add(part_a.at[at[3], s, :, back], from_a1.at[s, :, back])
        send(f"a2l{s}", part_a.at[at[3], s], from_a2.at[s, 1], left)

    def b2(s):
        receive(f"b1{s}2", from_b1.at[s, 2], across)
        add(part_b.at[at[2], s, y], from_b1.at[s, 2])
        send(f"b2r{s}", part_b.at[at[2], s, y, b_ways[0]], from_b2.at[s, b_ways[0]], right)
        send(f"b2l{s}", part_b.at[at[2], s, y, b_ways[1]], from_b2.at[s, b_ways[1]], left)

    def b3(s):
        go, back = b_ways
        receive(f"b1{s}1", from_b1.at[s, 1], across)
        receive(f"b2r{s}", from_b2.at[s, go], left)
        add(part_b.at[at[1], s, y, go], from_b1.at[s, 1, go], from_b2.at[s, go])
        add(part_b.at[at[1], s, y, back], from_b1.at[s, 1, back])
        send(f"b3r{s}", part_b.at[at[1], s, y], from_b3.at[s, 0], right)
        receive(f"b1{s}3", from_b1.at[s, 3], across)
        receive(f"b2l{s}", from_b2.at[s, back], right)
        add(part_b.at[at[3], s, y, go], from_b1.at[s, 3, go])
        add(part_b.at[at[3], s, y, back], from_b1.at[s, 3, back], from_b2.at[s, back])
        send(f"b3l{s}", part_b.at[at[3], s, y], from_b3.at[s, 1], left)

    def a3(s):
        receive(f"a2r{s}", from_a2.at[s, 0], left)
        receive(f"a2l{s}", from_a2.at[s, 1], right)
        add(part_a.at[at[0], s, mate], from_a2.at[s, 0, mate], from_a2.at[s, 1, mate])
        send(f"a3{s}", part_a.at[at[0], s, mate], from_a3.at[s], across)

    def rows_of(s, which):
        return (sub * s, a_rows) if which == 0 else (sub * s + a_rows, b_rows)

    met = []

    def update(s, which, sources):
        value = sources[0][...].astype(F32)
        for source in sources[1:]:
            value = value + source[...].astype(F32)
        start, count = rows_of(s, which)
        rows = slice(start, start + count)
        own = master[rows]
        column = gain_cols[rows]
        new = own - learn_rate * (value * jnp.concatenate([column, column], 1))
        upd[rows] = new
        payload[rows] = new.astype(BF16)
        if not met:
            meet_far()
            met.append(True)
        send(f"p{s}{which}", payload.at[pl.ds(start, count)], other.at[pl.ds(start, count)], ahead)
        both = own.astype(BF16).astype(F32) * value
        share[rows] = both[:, :128] + both[:, 128:]

    def b4(s):
        receive(f"b1{s}0", from_b1.at[s, 0], across)
        receive(f"b3r{s}", from_b3.at[s, 0], left)
        receive(f"b3l{s}", from_b3.at[s, 1], right)
        update(s, 1, [part_b.at[at[0], s, y], from_b1.at[s, 0], from_b3.at[s, 0], from_b3.at[s, 1]])

    def a4(s):
        receive(f"a3{s}", from_a3.at[s], across)
        update(
            s, 0,
            [part_a.at[at[0], s, y], from_a2.at[s, 0, y], from_a2.at[s, 1, y], from_a3.at[s]],
        )

    def gain_step():
        for k in range(shard // 128):
            block = slice(128 * k, 128 * k + 128)
            gradient = jnp.sum(share[block].T, 0, keepdims=True)
            upd_gain[:, block] = gains[:, block] - gain_rate * gradient
        gain_sent[...] = jnp.broadcast_to(upd_gain[...], (16, shard)).astype(BF16)
        send("gain", gain_sent, gain_other, ahead)

    written = []

    def average(s, which):
        start, count = rows_of(s, which)
        receive(f"p{s}{which}", other.at[pl.ds(start, count)], behind)
        rows = slice(start, start + count)
        new_weight[rows] = 0.5 * (upd[rows] + other[rows].astype(F32))
        rows = pl.ds(start, count)
        written.append(load(new_weight.at[rows], weight_out.at[0, rows], 19 + len(written)))

    def average_gain():
        receive("gain", gain_other, behind)
        upd_gain[...] = 0.5 * (upd_gain[...] + gain_other[...].astype(F32)[0:1])
        written.append(load(upd_gain, gain_out, 19 + len(written)))

    started = []

    def forward(j, q):
        value = jnp.dot(
            tok[at[j], rows_y[q]], whole_w[at[j], rows_y[q]], preferred_element_type=F32
        )
        total[...] = total[...] + value if started else value
        started.append(True)

    def gather_2y():
        receive("g1rb", whole_w.at[at[3], y, wb], left)
        move("g2yl", whole_w.at[at[3], y, wb], across)
        receive("g1lb", whole_w.at[at[1], y, wb], right)
        move("g2yr", whole_w.at[at[1], y, wb], across)

    def gather_2b():
        receive("g1rb", whole_w.at[at[3], y, wb], left)
        move("g2rb", whole_w.at[at[3], y, wb_ways[0]], right)
        receive("g1lb", whole_w.at[at[1], y, wb], right)
        move("g2lb", whole_w.at[at[1], y, wb_ways[1]], left)

    def gather_2a():
        receive("g1ra", whole_w.at[at[3], y, wa], left)
        move("g2ra", whole_w.at[at[3], y, wa_ways[0]], right)
        receive("g1la", whole_w.at[at[1], y, wa], right)
        move("g2la", whole_w.at[at[1], y, wa_ways[1]], left)

    def gather_2p():
        receive("g1ya", whole_w.at[x, mate, wa], across)
        move("g2pr", whole_w.at[x, mate, wa], right)
        move("g2pl", whole_w.at[x, mate, wa], left)

    def gather_3y():
        receive("g2rb", whole_w.at[at[2], y, wb_ways[0]], left)
        receive("g2lb", whole_w.at[at[2], y, wb_ways[1]], right)
        move("g3y", whole_w.at[at[2], y, wb], across)

    def gather_3x():
        receive("g2pr", whole_w.at[at[3], mate, wa], left)
        move("g3r", whole_w.at[at[3], mate, wa_ways[0]], right)
        receive("g2pl", whole_w.at[at[1], mate, wa], right)
        move("g3l", whole_w.at[at[1], mate, wa_ways[1]], left)

    def f00():
        forward(0, 0)

    def f01():
        receive("g1yb", whole_w.at[x, mate, wb], across)
        receive("g1ya", whole_w.at[x, mate, wa], across)
        forward(0, 1)

    def f10():
        receive("g1lb", whole_w.at[at[1], y, wb], right)
        receive("g1la", whole_w.at[at[1], y, wa], right)
        forward(1, 0)

    def f30():
        receive("g1rb", whole_w.at[at[3], y, wb], left)
        receive("g1ra", whole_w.at[at[3], y, wa], left)
        forward(3, 0)

    def f20():
        receive("g2rb", whole_w.at[at[2], y, wb_ways[0]], left)
        receive("g2lb", whole_w.at[at[2], y, wb_ways[1]], right)
        receive("g2ra", whole_w.at[at[2], y, wa_ways[0]], left)
        receive("g2la", whole_w.at[at[2], y, wa_ways[1]], right)
        forward(2, 0)

    def f31():
        receive("g2yl", whole_w.at[at[3], mate, wb], across)
        receive("g2pr", whole_w.at[at[3], mate, wa], left)
        forward(3, 1)

    def f11():
        receive("g2yr", whole_w.at[at[1], mate, wb], across)
        receive("g2pl", whole_w.at[at[1], mate, wa], right)
        forward(1, 1)

    def f21():
        receive("g3r", whole_w.at[at[2], mate, wa_ways[0]], left)
        receive("g3l", whole_w.at[at[2], mate, wa_ways[1]], right)
        receive("g3y", whole_w.at[at[2], mate, wb], across)
        forward(2, 1)

    def out():
        send("out", total.at[theirs], from_sibling, sibling)

    def finish():
        receive("out", from_sibling, sibling)
        factor = inverse[...]
        new_kv[...] = (
            (total[0:n_tok] + from_sibling[...]) * jnp.concatenate([factor, factor], 1)
        ).astype(BF16)
        written.append(load(new_kv, kv_out, 19 + len(written)))

    part = functools.partial
    steps = dict(
        g1ya=part(gather_1y, "a", wa), g1yb=part(gather_1y, "b", wb),
        g1xa=part(gather_1x, "a", wa), g1xb=part(gather_1x, "b", wb),
        t_0_first=part(send_tokens, 0, (2,)), t_0_rest=part(send_tokens, 0, (1, 3, 0)),
        t_1=part(send_tokens, 1, (2, 1, 3, 0)),
        norm=norm, scaled=scale_cotangent,
        p_0_first=part(product, 0, (2,)), p_0_rest=part(product, 0, (1, 3, 0)),
        g2y=gather_2y, g2a=gather_2a, g2b=gather_2b, g2p=gather_2p, g3y=gather_3y, g3x=gather_3x,
        f00=f00, f01=f01, f10=f10, f30=f30, f20=f20, f31=f31, f11=f11, f21=f21,
        gain=gain_step, out=out, average_gain=average_gain, finish=finish,
    )
    for s in range(n_sub):
        for name, step in (("a2", a2), ("b2", b2), ("b3", b3), ("a3", a3), ("a4", a4), ("b4", b4)):
            steps[f"{name}_{s}"] = functools.partial(step, s)
        if s:
            steps[f"p_{s}"] = functools.partial(product, s, (2, 1, 3, 0))
        for which in range(2):
            steps[f"av_{s}{which}"] = functools.partial(average, s, which)
    for name in schedule:
        steps[name]()
    for copy in list(sent.values()):
        copy.wait_send()
    for copy in written:
        copy.wait()
    assert done == set(sent)


def step_at(distance, collective, n_rep, tokens, cotangent, weight, gain, plan=None):
    plan = plan or (FAR if distance >= 8 else NEAR if distance > 1 else NEXT)
    n_sub, split = plan[:2]
    n_tok, width = tokens.shape
    _, shard, kv = weight.shape
    a_rows, b_rows = split[0] + split[1], split[2] + split[3]
    any_space = pl.BlockSpec(memory_space=pl.ANY)
    return pl.pallas_call(
        functools.partial(kernel, distance, n_rep, plan),
        out_shape=(
            jax.ShapeDtypeStruct((n_tok, kv), BF16),
            jax.ShapeDtypeStruct(weight.shape, F32),
            jax.ShapeDtypeStruct(gain.shape, F32),
        ),
        in_specs=[any_space] * 4,
        out_specs=(any_space,) * 3,
        scratch_shapes=[
            pltpu.VMEM((4, 2, 2 * n_tok, shard), BF16),
            pltpu.VMEM((8, n_tok, shard), BF16),
            pltpu.VMEM((n_tok, kv), BF16),
            pltpu.VMEM((shard, kv), F32),
            pltpu.VMEM((1, shard), F32),
            pltpu.VMEM((shard, 128), F32),
            pltpu.VMEM((2 * n_tok, kv), BF16),
            pltpu.VMEM((n_tok, 128), F32),
            pltpu.VMEM((4, n_sub, 2, a_rows, kv), BF16),
            pltpu.VMEM((4, n_sub, 2, b_rows, kv), BF16),
            pltpu.VMEM((4, 2, shard, kv), BF16),
            pltpu.VMEM((n_sub, 2, a_rows, kv), BF16),
            pltpu.VMEM((n_sub, 2, 2, a_rows, kv), BF16),
            pltpu.VMEM((n_sub, a_rows, kv), BF16),
            pltpu.VMEM((n_sub, 4, b_rows, kv), BF16),
            pltpu.VMEM((n_sub, b_rows, kv), BF16),
            pltpu.VMEM((n_sub, 2, b_rows, kv), BF16),
            pltpu.VMEM((shard, kv), BF16),
            pltpu.VMEM((shard, kv), BF16),
            pltpu.VMEM((shard, 128), F32),
            pltpu.VMEM((shard, kv), F32),
            pltpu.VMEM((1, shard), F32),
            pltpu.VMEM((shard, kv), F32),
            pltpu.VMEM((n_tok, kv), BF16),
            pltpu.VMEM((16, shard), BF16),
            pltpu.VMEM((16, shard), BF16),
            pltpu.VMEM((2 * n_tok, kv), F32),
            pltpu.VMEM((n_tok, kv), F32),
            pltpu.SemaphoreType.REGULAR((2,)),
            pltpu.SemaphoreType.DMA((19 + 2 * n_sub + 2,)),
            pltpu.SemaphoreType.DMA((MESSAGES,)),
            pltpu.SemaphoreType.DMA((MESSAGES,)),
        ],
        compiler_params=pltpu.CompilerParams(
            collective_id=collective, has_side_effects=True, vmem_limit_bytes=48 * 2**20
        ),
        name=f"step_{distance}",
    )(tokens, cotangent, weight, gain)


def hand_over_kernel(*refs):
    sources, targets, semaphores = refs[:3], refs[3:6], refs[6]
    copies = [
        pltpu.make_async_copy(source, target, semaphores.at[i])
        for i, (source, target) in enumerate(zip(sources, targets))
    ]
    for copy in copies:
        copy.start()
    for copy in copies:
        copy.wait()


def hand_over(*arrays):
    any_space = pl.BlockSpec(memory_space=pl.ANY)
    return pl.pallas_call(
        hand_over_kernel,
        out_shape=tuple(jax.ShapeDtypeStruct(a.shape, a.dtype) for a in arrays),
        in_specs=[any_space] * 3,
        out_specs=(any_space,) * 3,
        scratch_shapes=[pltpu.SemaphoreType.DMA((3,))],
        name="hand_over",
    )(*arrays)


def body(tokens, cotangent, weight, gain, step):
    n_rep = lax.axis_size("rep")
    levels = n_rep.bit_length() - 1
    branches = [functools.partial(step_at, 1 << bit, bit, n_rep) for bit in range(levels)]
    return hand_over(*lax.switch(step % levels, branches, tokens, cotangent, weight, gain))


def solution(mesh):
    return jax.shard_map(
        body,
        mesh=mesh,
        in_specs=(
            P(("rep", "fsdp"), None),
            P(("rep", "fsdp"), None),
            P("rep", "fsdp", None),
            P("rep", "fsdp"),
            P(),
        ),
        out_specs=(P(("rep", "fsdp"), None), P("rep", "fsdp", None), P("rep", "fsdp")),
        check_vma=False,
    )
```

```python
import functools

import jax
import jax.numpy as jnp
from jax import lax
from jax.experimental import pallas as pl
from jax.experimental.pallas import tpu as pltpu
from jax.sharding import PartitionSpec as P

learn_rate = 0.25
gain_rate = 0.01
MESH = pl.DeviceIdType.MESH
F32, BF16 = jnp.float32, jnp.bfloat16
MESSAGES = 128
NEAR_STEPS = (
    "meet", "g1ya", "g1xb", "t_0_first", "t_0_rest", "norm", "scaled", "cot", "t_1", "p_0_first", "p_0_rest",
    "p_1", "a2_0", "b2_0", "a2_1", "b3_0", "b2_1", "a3_0", "b4_0", "b3_1", "a3_1", "g1xa", "g1yb", "g2b",
    "g2y", "g2p", "a4_0", "b4_1", "a4_1", "gain", "g2a", "g3y", "g3x", "f00", "f10", "f30", "f01", "f20",
    "f31", "f11", "f21", "out", "av_01", "av_00", "av_11", "av_10", "average_gain", "finish",
)
FAR_STEPS = (
    "meet", "t_0_first", "norm", "scaled", "cot", "t_0_rest", "t_1", "p_0_first", "p_0_rest", "p_1", "b2_0",
    "a2_0", "p_2", "b2_1", "a2_1", "p_3", "b3_0", "a3_0", "b2_2", "a2_2", "b4_0", "b3_1", "a3_1", "a4_0",
    "b2_3", "a2_3", "b4_1", "b3_2", "a3_2", "a4_1", "b3_3", "a3_3", "b4_2", "a4_2", "g1ya", "g1xb", "g1xa",
    "g1yb", "b4_3", "a4_3", "gain", "g2b", "g2y", "g2p", "g2a", "g3y", "g3x", "f00", "f10", "f30", "f01",
    "f20", "f31", "f11", "f21", "out", "av_01", "av_00", "av_11", "av_10", "av_21", "av_20", "av_31", "av_30",
    "average_gain", "finish",
)
NEXT = (2, (80, 80, 48, 48), (352, 160), NEAR_STEPS)
NEAR = (2, (64, 64, 64, 64), (256, 256), NEAR_STEPS)
FAR = (4, (48, 32, 16, 32), (288, 224), FAR_STEPS)


def kernel(
    distance, n_rep, plan, tokens, cotangent, weight, gain, kv_out, weight_out, gain_out,
    tok, tok_rest, cot, master, gains, gain_cols, scaled, inverse, part_a, part_b, whole_w,
    from_a1, from_a2, from_a3, from_b1, from_b2, from_b3, payload, other, share, upd, upd_gain, new_weight, new_kv,
    gain_sent, gain_other, total, from_sibling, meeting, local_sem, send_sem, recv_sem,
):
    n_sub, split, (wa_rows, wb_rows), schedule = plan
    rep, fsdp = lax.axis_index("rep"), lax.axis_index("fsdp")
    n_fsdp = lax.axis_size("fsdp")
    x, y, core = fsdp // 4, (fsdp // 2) % 2, fsdp % 2
    mate = 1 - y
    sibling = (rep, fsdp + 1 - 2 * core)
    across = (rep, fsdp + 2 - 4 * y)
    right = (rep, (fsdp + 4) % n_fsdp)
    left = (rep, (fsdp + n_fsdp - 4) % n_fsdp)
    ahead = ((rep + distance) % n_rep, fsdp)
    behind = ((rep + n_rep - distance) % n_rep, fsdp)
    at = [(x + j) % 4 for j in range(4)]
    rows_y = (y, mate)
    n_tok = cotangent.shape[0]
    width = tokens.shape[1]
    shard, kv = master.shape
    sub = shard // n_sub
    token_part = max(sub, shard // 2)
    a_rows, b_rows = split[0] + split[1], split[2] + split[3]
    a_ways = (pl.ds(0, split[0]), pl.ds(split[0], split[1]))
    b_ways = (pl.ds(0, split[2]), pl.ds(split[2], split[3]))
    wa, wb = pl.ds(0, wa_rows), pl.ds(wa_rows, wb_rows)
    wa_ways = (pl.ds(0, wa_rows // 2), pl.ds(wa_rows // 2, wa_rows // 2))
    wb_ways = (pl.ds(wa_rows, wb_rows // 2), pl.ds(wa_rows + wb_rows // 2, wb_rows // 2))
    scale = width**-0.5
    theirs = pl.ds(n_tok, n_tok)

    barrier = pltpu.get_barrier_semaphore()
    first, second = fsdp - core, fsdp - core + 1

    def greet(device):
        pl.semaphore_signal(barrier, inc=1, device_id=device, device_id_type=MESH)

    @pl.when(core == 1)
    def _():
        greet((rep, first))

    for f in ((first + 2 - 4 * y), (first + 4) % n_fsdp, (first + n_fsdp - 4) % n_fsdp):
        greet((rep, f))
    greet((ahead[0], second))
    greet((behind[0], second))

    def tell(semaphore):
        pl.semaphore_signal(semaphore, inc=1, device_id=sibling, device_id_type=MESH)

    def meet_group():
        @pl.when(core == 0)
        def _():
            pl.semaphore_wait(barrier, 7)
            tell(meeting.at[0])

        @pl.when(core == 1)
        def _():
            pl.semaphore_wait(meeting.at[0], 1)

    def meet_far():
        @pl.when(core == 1)
        def _():
            pl.semaphore_wait(barrier, 4)
            tell(meeting.at[1])

        @pl.when(core == 0)
        def _():
            pl.semaphore_wait(meeting.at[1], 1)

    def load(source, target, index):
        copy = pltpu.make_async_copy(source, target, local_sem.at[index])
        copy.start()
        return copy

    load_w = load(weight.at[0], master, 0)
    load_g = load(gain, gains, 1)
    load_c = load(cotangent, cot, 2)
    load_t = []
    for block in range(8):
        for mine in (True, False):
            column = 1024 * block + 512 * (core if mine else 1 - core)
            source = tokens.at[:, pl.ds(pl.multiple_of(column, 512), 512)]
            target = tok.at[block // 2, block % 2, pl.ds(0, n_tok)] if mine else tok_rest.at[block]
            load_t.append((load(source, target, 3 + len(load_t)), target))

    names = {}
    sent = {}
    done = set()

    def message(name, source, target, device):
        index = names.setdefault(name, len(names))
        assert index < MESSAGES
        return pltpu.make_async_remote_copy(
            src_ref=source, dst_ref=target, send_sem=send_sem.at[index],
            recv_sem=recv_sem.at[index], device_id=device, device_id_type=MESH,
        )

    def send(name, source, target, device):
        sent[name] = message(name, source, target, device)
        sent[name].start()

    def receive(name, target, device):
        if name not in done:
            done.add(name)
            message(name, target, target, device).wait_recv()

    load_w.wait()
    load_g.wait()
    gb_row = gains[...].astype(BF16).astype(F32)
    for k in range(shard // 128):
        block = slice(128 * k, 128 * k + 128)
        gain_cols[block] = jnp.broadcast_to(gb_row[:, block], (128, 128)).T
        wb_block = master[block].astype(BF16).astype(F32)
        column = gain_cols[block]
        whole_w[x, y, block] = (wb_block * jnp.concatenate([column, column], 1)).astype(BF16)

    def move(name, ref, device):
        send(name, ref, ref, device)

    def gather_1y(part, rows):
        move("g1y" + part, whole_w.at[x, y, rows], across)

    def gather_1x(part, rows):
        move("g1r" + part, whole_w.at[x, y, rows], right)
        move("g1l" + part, whole_w.at[x, y, rows], left)

    def send_tokens(s, chips):
        for j, q in [(j, q) for j in chips for q in (1, 0)]:
            column = 512 * (4 * at[j] + 2 * rows_y[q] + 1 - core) + token_part * s
            send(
                f"t{s}{j}{q}", tokens.at[:, pl.ds(pl.multiple_of(column, token_part), token_part)],
                tok.at[at[j], rows_y[q], theirs, pl.ds(token_part * s, token_part)], sibling,
            )

    def norm():
        squares = jnp.zeros((n_tok, 128), F32)
        for copy, target in load_t:
            copy.wait()
            for k in range(4):
                value = target[:, 128 * k : 128 * k + 128].astype(F32)
                squares = squares + value * value
        mean = jnp.sum(squares, 1, keepdims=True) * (1.0 / width)
        inverse[...] = jnp.broadcast_to(lax.rsqrt(mean + 1e-05) * scale, (n_tok, 128))

    def scale_cotangent():
        load_c.wait()
        factor = inverse[...]
        scaled[0:n_tok] = (cot[...].astype(F32) * jnp.concatenate([factor, factor], 1)).astype(BF16)

    def send_cotangent():
        send("cot", scaled.at[pl.ds(0, n_tok)], scaled.at[theirs], sibling)

    def product(s, chips):
        columns = pl.ds(sub * s, sub)
        receive("cot", scaled.at[theirs], sibling)
        for j in chips:
            for q in (1, 0):
                h = sub * s // token_part
                half = pl.ds(token_part * h, token_part)
                receive(f"t{h}{j}{q}", tok.at[at[j], rows_y[q], theirs, half], sibling)
        for j in chips:
            for q in (1, 0):
                value = lax.dot_general(
                    tok[at[j], rows_y[q], :, columns], scaled[...], (((0,), (0,)), ((), ())),
                    preferred_element_type=F32,
                ).astype(BF16)
                part_a[at[j], s, rows_y[q]] = value[:a_rows]
                part_b[at[j], s, rows_y[q]] = value[a_rows:]
        for j in chips:
            send(f"b1{s}{j}", part_b.at[at[j], s, mate], from_b1.at[s, j], across)
            if j == 2:
                send(f"a1r{s}", part_a.at[at[2], s, :, a_ways[0]], from_a1.at[s, :, a_ways[0]], right)
                send(f"a1l{s}", part_a.at[at[2], s, :, a_ways[1]], from_a1.at[s, :, a_ways[1]], left)

    def add(target, *sources):
        value = target[...].astype(F32)
        for source in sources:
            value = value + source[...].astype(F32)
        target[...] = value.astype(BF16)

    def a2(s):
        go, back = a_ways
        receive(f"a1r{s}", from_a1.at[s, :, go], left)
        add(part_a.at[at[1], s, :, go], from_a1.at[s, :, go])
        send(f"a2r{s}", part_a.at[at[1], s], from_a2.at[s, 0], right)
        receive(f"a1l{s}", from_a1.at[s, :, back], right)
        add(part_a.at[at[3], s, :, back], from_a1.at[s, :, back])
        send(f"a2l{s}", part_a.at[at[3], s], from_a2.at[s, 1], left)

    def b2(s):
        receive(f"b1{s}2", from_b1.at[s, 2], across)
        add(part_b.at[at[2], s, y], from_b1.at[s, 2])
        send(f"b2r{s}", part_b.at[at[2], s, y, b_ways[0]], from_b2.at[s, b_ways[0]], right)
        send(f"b2l{s}", part_b.at[at[2], s, y, b_ways[1]], from_b2.at[s, b_ways[1]], left)

    def b3(s):
        go, back = b_ways
        receive(f"b1{s}1", from_b1.at[s, 1], across)
        receive(f"b2r{s}", from_b2.at[s, go], left)
        add(part_b.at[at[1], s, y, go], from_b1.at[s, 1, go], from_b2.at[s, go])
        add(part_b.at[at[1], s, y, back], from_b1.at[s, 1, back])
        send(f"b3r{s}", part_b.at[at[1], s, y], from_b3.at[s, 0], right)
        receive(f"b1{s}3", from_b1.at[s, 3], across)
        receive(f"b2l{s}", from_b2.at[s, back], right)
        add(part_b.at[at[3], s, y, go], from_b1.at[s, 3, go])
        add(part_b.at[at[3], s, y, back], from_b1.at[s, 3, back], from_b2.at[s, back])
        send(f"b3l{s}", part_b.at[at[3], s, y], from_b3.at[s, 1], left)

    def a3(s):
        receive(f"a2r{s}", from_a2.at[s, 0], left)
        receive(f"a2l{s}", from_a2.at[s, 1], right)
        add(part_a.at[at[0], s, mate], from_a2.at[s, 0, mate], from_a2.at[s, 1, mate])
        send(f"a3{s}", part_a.at[at[0], s, mate], from_a3.at[s], across)

    def rows_of(s, which):
        return (sub * s, a_rows) if which == 0 else (sub * s + a_rows, b_rows)

    met = []

    def update(s, which, sources):
        value = sources[0][...].astype(F32)
        for source in sources[1:]:
            value = value + source[...].astype(F32)
        start, count = rows_of(s, which)
        rows = slice(start, start + count)
        own = master[rows]
        column = gain_cols[rows]
        new = own - learn_rate * (value * jnp.concatenate([column, column], 1))
        upd[rows] = new
        payload[rows] = new.astype(BF16)
        if not met:
            meet_far()
            met.append(True)
        send(f"p{s}{which}", payload.at[pl.ds(start, count)], other.at[pl.ds(start, count)], ahead)
        both = own.astype(BF16).astype(F32) * value
        share[rows] = both[:, :128] + both[:, 128:]

    def b4(s):
        receive(f"b1{s}0", from_b1.at[s, 0], across)
        receive(f"b3r{s}", from_b3.at[s, 0], left)
        receive(f"b3l{s}", from_b3.at[s, 1], right)
        update(s, 1, [part_b.at[at[0], s, y], from_b1.at[s, 0], from_b3.at[s, 0], from_b3.at[s, 1]])

    def a4(s):
        receive(f"a3{s}", from_a3.at[s], across)
        update(
            s, 0,
            [part_a.at[at[0], s, y], from_a2.at[s, 0, y], from_a2.at[s, 1, y], from_a3.at[s]],
        )

    def gain_step():
        for k in range(shard // 128):
            block = slice(128 * k, 128 * k + 128)
            gradient = jnp.sum(share[block].T, 0, keepdims=True)
            upd_gain[:, block] = gains[:, block] - gain_rate * gradient
        gain_sent[...] = jnp.broadcast_to(upd_gain[...], (16, shard)).astype(BF16)
        send("gain", gain_sent, gain_other, ahead)

    written = []

    def average(s, which):
        start, count = rows_of(s, which)
        receive(f"p{s}{which}", other.at[pl.ds(start, count)], behind)
        rows = slice(start, start + count)
        new_weight[rows] = 0.5 * (upd[rows] + other[rows].astype(F32))
        rows = pl.ds(start, count)
        written.append(load(new_weight.at[rows], weight_out.at[0, rows], 19 + len(written)))

    def average_gain():
        receive("gain", gain_other, behind)
        upd_gain[...] = 0.5 * (upd_gain[...] + gain_other[...].astype(F32)[0:1])
        written.append(load(upd_gain, gain_out, 19 + len(written)))

    started = []

    def forward(j, q):
        value = jnp.dot(
            tok[at[j], rows_y[q]], whole_w[at[j], rows_y[q]], preferred_element_type=F32
        )
        total[...] = total[...] + value if started else value
        started.append(True)

    def gather_2y():
        receive("g1rb", whole_w.at[at[3], y, wb], left)
        move("g2yl", whole_w.at[at[3], y, wb], across)
        receive("g1lb", whole_w.at[at[1], y, wb], right)
        move("g2yr", whole_w.at[at[1], y, wb], across)

    def gather_2b():
        receive("g1rb", whole_w.at[at[3], y, wb], left)
        move("g2rb", whole_w.at[at[3], y, wb_ways[0]], right)
        receive("g1lb", whole_w.at[at[1], y, wb], right)
        move("g2lb", whole_w.at[at[1], y, wb_ways[1]], left)

    def gather_2a():
        receive("g1ra", whole_w.at[at[3], y, wa], left)
        move("g2ra", whole_w.at[at[3], y, wa_ways[0]], right)
        receive("g1la", whole_w.at[at[1], y, wa], right)
        move("g2la", whole_w.at[at[1], y, wa_ways[1]], left)

    def gather_2p():
        receive("g1ya", whole_w.at[x, mate, wa], across)
        move("g2pr", whole_w.at[x, mate, wa], right)
        move("g2pl", whole_w.at[x, mate, wa], left)

    def gather_3y():
        receive("g2rb", whole_w.at[at[2], y, wb_ways[0]], left)
        receive("g2lb", whole_w.at[at[2], y, wb_ways[1]], right)
        move("g3y", whole_w.at[at[2], y, wb], across)

    def gather_3x():
        receive("g2pr", whole_w.at[at[3], mate, wa], left)
        move("g3r", whole_w.at[at[3], mate, wa_ways[0]], right)
        receive("g2pl", whole_w.at[at[1], mate, wa], right)
        move("g3l", whole_w.at[at[1], mate, wa_ways[1]], left)

    def f00():
        forward(0, 0)

    def f01():
        receive("g1yb", whole_w.at[x, mate, wb], across)
        receive("g1ya", whole_w.at[x, mate, wa], across)
        forward(0, 1)

    def f10():
        receive("g1lb", whole_w.at[at[1], y, wb], right)
        receive("g1la", whole_w.at[at[1], y, wa], right)
        forward(1, 0)

    def f30():
        receive("g1rb", whole_w.at[at[3], y, wb], left)
        receive("g1ra", whole_w.at[at[3], y, wa], left)
        forward(3, 0)

    def f20():
        receive("g2rb", whole_w.at[at[2], y, wb_ways[0]], left)
        receive("g2lb", whole_w.at[at[2], y, wb_ways[1]], right)
        receive("g2ra", whole_w.at[at[2], y, wa_ways[0]], left)
        receive("g2la", whole_w.at[at[2], y, wa_ways[1]], right)
        forward(2, 0)

    def f31():
        receive("g2yl", whole_w.at[at[3], mate, wb], across)
        receive("g2pr", whole_w.at[at[3], mate, wa], left)
        forward(3, 1)

    def f11():
        receive("g2yr", whole_w.at[at[1], mate, wb], across)
        receive("g2pl", whole_w.at[at[1], mate, wa], right)
        forward(1, 1)

    def f21():
        receive("g3r", whole_w.at[at[2], mate, wa_ways[0]], left)
        receive("g3l", whole_w.at[at[2], mate, wa_ways[1]], right)
        receive("g3y", whole_w.at[at[2], mate, wb], across)
        forward(2, 1)

    def out():
        send("out", total.at[theirs], from_sibling, sibling)

    def finish():
        receive("out", from_sibling, sibling)
        factor = inverse[...]
        new_kv[...] = (
            (total[0:n_tok] + from_sibling[...]) * jnp.concatenate([factor, factor], 1)
        ).astype(BF16)
        written.append(load(new_kv, kv_out, 19 + len(written)))

    part = functools.partial
    steps = dict(
        g1ya=part(gather_1y, "a", wa), g1yb=part(gather_1y, "b", wb),
        g1xa=part(gather_1x, "a", wa), g1xb=part(gather_1x, "b", wb),
        t_0_first=part(send_tokens, 0, (2,)), t_0_rest=part(send_tokens, 0, (1, 3, 0)),
        t_1=part(send_tokens, 1, (2, 1, 3, 0)),
        norm=norm, scaled=scale_cotangent, meet=meet_group, cot=send_cotangent,
        p_0_first=part(product, 0, (2,)), p_0_rest=part(product, 0, (1, 3, 0)),
        g2y=gather_2y, g2a=gather_2a, g2b=gather_2b, g2p=gather_2p, g3y=gather_3y, g3x=gather_3x,
        f00=f00, f01=f01, f10=f10, f30=f30, f20=f20, f31=f31, f11=f11, f21=f21,
        gain=gain_step, out=out, average_gain=average_gain, finish=finish,
    )
    for s in range(n_sub):
        for name, step in (("a2", a2), ("b2", b2), ("b3", b3), ("a3", a3), ("a4", a4), ("b4", b4)):
            steps[f"{name}_{s}"] = functools.partial(step, s)
        if s:
            steps[f"p_{s}"] = functools.partial(product, s, (2, 1, 3, 0))
        for which in range(2):
            steps[f"av_{s}{which}"] = functools.partial(average, s, which)
    for name in schedule:
        steps[name]()
    for copy in list(sent.values()):
        copy.wait_send()
    for copy in written:
        copy.wait()
    assert done == set(sent)


def step_at(distance, collective, n_rep, tokens, cotangent, weight, gain, plan=None):
    plan = plan or (FAR if distance >= 8 else NEAR if distance > 1 else NEXT)
    n_sub, split = plan[:2]
    n_tok, width = tokens.shape
    _, shard, kv = weight.shape
    a_rows, b_rows = split[0] + split[1], split[2] + split[3]
    any_space = pl.BlockSpec(memory_space=pl.ANY)
    return pl.pallas_call(
        functools.partial(kernel, distance, n_rep, plan),
        out_shape=(
            jax.ShapeDtypeStruct((n_tok, kv), BF16),
            jax.ShapeDtypeStruct(weight.shape, F32),
            jax.ShapeDtypeStruct(gain.shape, F32),
        ),
        in_specs=[any_space] * 4,
        out_specs=(any_space,) * 3,
        scratch_shapes=[
            pltpu.VMEM((4, 2, 2 * n_tok, shard), BF16),
            pltpu.VMEM((8, n_tok, shard), BF16),
            pltpu.VMEM((n_tok, kv), BF16),
            pltpu.VMEM((shard, kv), F32),
            pltpu.VMEM((1, shard), F32),
            pltpu.VMEM((shard, 128), F32),
            pltpu.VMEM((2 * n_tok, kv), BF16),
            pltpu.VMEM((n_tok, 128), F32),
            pltpu.VMEM((4, n_sub, 2, a_rows, kv), BF16),
            pltpu.VMEM((4, n_sub, 2, b_rows, kv), BF16),
            pltpu.VMEM((4, 2, shard, kv), BF16),
            pltpu.VMEM((n_sub, 2, a_rows, kv), BF16),
            pltpu.VMEM((n_sub, 2, 2, a_rows, kv), BF16),
            pltpu.VMEM((n_sub, a_rows, kv), BF16),
            pltpu.VMEM((n_sub, 4, b_rows, kv), BF16),
            pltpu.VMEM((n_sub, b_rows, kv), BF16),
            pltpu.VMEM((n_sub, 2, b_rows, kv), BF16),
            pltpu.VMEM((shard, kv), BF16),
            pltpu.VMEM((shard, kv), BF16),
            pltpu.VMEM((shard, 128), F32),
            pltpu.VMEM((shard, kv), F32),
            pltpu.VMEM((1, shard), F32),
            pltpu.VMEM((shard, kv), F32),
            pltpu.VMEM((n_tok, kv), BF16),
            pltpu.VMEM((16, shard), BF16),
            pltpu.VMEM((16, shard), BF16),
            pltpu.VMEM((2 * n_tok, kv), F32),
            pltpu.VMEM((n_tok, kv), F32),
            pltpu.SemaphoreType.REGULAR((2,)),
            pltpu.SemaphoreType.DMA((19 + 2 * n_sub + 2,)),
            pltpu.SemaphoreType.DMA((MESSAGES,)),
            pltpu.SemaphoreType.DMA((MESSAGES,)),
        ],
        compiler_params=pltpu.CompilerParams(
            collective_id=collective, has_side_effects=True, vmem_limit_bytes=48 * 2**20
        ),
        name=f"step_{distance}",
    )(tokens, cotangent, weight, gain)


def hand_over_kernel(*refs):
    sources, targets, semaphores = refs[:3], refs[3:6], refs[6]
    copies = [
        pltpu.make_async_copy(source, target, semaphores.at[i])
        for i, (source, target) in enumerate(zip(sources, targets))
    ]
    for copy in copies:
        copy.start()
    for copy in copies:
        copy.wait()


def hand_over(*arrays):
    any_space = pl.BlockSpec(memory_space=pl.ANY)
    return pl.pallas_call(
        hand_over_kernel,
        out_shape=tuple(jax.ShapeDtypeStruct(a.shape, a.dtype) for a in arrays),
        in_specs=[any_space] * 3,
        out_specs=(any_space,) * 3,
        scratch_shapes=[pltpu.SemaphoreType.DMA((3,))],
        name="hand_over",
    )(*arrays)


def body(tokens, cotangent, weight, gain, step):
    n_rep = lax.axis_size("rep")
    levels = n_rep.bit_length() - 1
    branches = [functools.partial(step_at, 1 << bit, bit, n_rep) for bit in range(levels)]
    return hand_over(*lax.switch(step % levels, branches, tokens, cotangent, weight, gain))


def solution(mesh):
    return jax.shard_map(
        body,
        mesh=mesh,
        in_specs=(
            P(("rep", "fsdp"), None),
            P(("rep", "fsdp"), None),
            P("rep", "fsdp", None),
            P("rep", "fsdp"),
            P(),
        ),
        out_specs=(P(("rep", "fsdp"), None), P("rep", "fsdp", None), P("rep", "fsdp")),
        check_vma=False,
    )
```
